32 devices in a mesh: seq: 8 (over z, x), head: 4 (over y, core).
Axes of the slice: x: 2, y: 2, z: 4, core: 2. Of those that a mesh axis runs over, the one named last changes fastest.
Arguments:
- cached_probs: bfloat16 [32, 40, 8, 128, 128], P('seq', 'head'), may hold values from 0 to 1, as said below
- out_old: bfloat16 [4096, 5120], P('seq', 'head'), may hold values from -6 to 6
- key_lists: int32 [32, 8], P('seq'), may hold values from 0 to 31, as said below
- changed_block_numbers: int32 [8], replicated, may hold values from 0 to 31, as said below
- delta_v: bfloat16 [1024, 1024], P('seq', 'head'), may hold values from -24 to 24
- w_out: bfloat16 [5120, 5120], P('head', 'seq'), may hold values from -0.078125 to 0.078125
Outputs:
- attn_new: bfloat16 [4096, 5120], P('seq', 'head')
- out_proj: bfloat16 [4096, 5120], P('seq', 'head')
The draws below stay inside these ranges and needn't reach their ends.
Inputs may be any that keep to these rules, and one draw needn't show every extreme that they name: `changed_block_numbers`: the changed block numbers are all different; the first block and the last block are always among them. `key_lists`: each query block lists 8 different key blocks; some list many changed blocks, most list few. `cached_probs`: for each query block, head and row, the weights over the row's listed keys are positive and sum to at most 1.
All inputs are finite; a program needn't handle non-finite values.
Results may differ from the reference program's by a relative error of at most 0.017.
Values may be sent and summed in bfloat16 or wider, within the bound.
No kernel may reach another device: no remote copies, remote signals or barrier semaphores. Data moves between devices by JAX's collectives and lax.ppermute only.
A program may use at most 128 MiB of HBM per device.

```python
import jax
import jax.numpy as jnp
from jax import lax

D = 5120
HQ = 40
KVH = 8
HD = 128
BLK = 128
TOP_KEY_BLOCKS = 8
GROUP = 5
HQ_DEV = 10
TOKENS = 4096
NB = 32
NCB = 8
N_HEAD = 4


def pick_changed(key):
    middle = jax.random.permutation(jax.random.fold_in(key, 11), NB - 2)[:NCB - 2].astype(jnp.int32) + 1
    ends = jnp.array([0, NB - 1], jnp.int32)
    chosen = jnp.concatenate([ends, middle])
    return jax.random.permutation(jax.random.fold_in(key, 12), chosen).astype(jnp.int32)


def draw_changed_block_numbers(key, part):
    return pick_changed(key)


def draw_cached_probs(key, part):
    block_keys = jax.random.split(jax.random.fold_in(key, 31), NB)

    def one_block(block_key):
        logit_key, share_key = jax.random.split(block_key, 2)
        logits = 2.5 * jax.random.normal(logit_key, (HQ, TOP_KEY_BLOCKS, BLK, BLK), jnp.float32)
        weights = jax.nn.softmax(logits, axis=(1, 3))
        share = jax.random.uniform(share_key, (HQ, 1, BLK, 1), jnp.float32, 0.5, 1.0)
        return (weights * share).astype(jnp.bfloat16)
    return lax.map(one_block, block_keys)


def draw_key_lists(key, part):
    changed = pick_changed(key)
    marked = jnp.zeros((NB,), jnp.int32).at[changed].set(1)
    ordered = jnp.argsort(marked, stable=True).astype(jnp.int32)
    unchanged = ordered[:NB - NCB]
    row_keys = jax.random.split(jax.random.fold_in(key, 23), NB)

    def one_row(row_key):
        partition_keys = jax.random.split(row_key, 6)
        baseline_count = jax.random.randint(partition_keys[0], (), 0, 3)
        spike_enabled = (jax.random.randint(partition_keys[1], (), 0, 4) == 0).astype(jnp.int32)
        spike_count = spike_enabled * jax.random.randint(partition_keys[2], (), 0, TOP_KEY_BLOCKS + 1)
        total_count = jnp.minimum(baseline_count + spike_count, TOP_KEY_BLOCKS)
        from_changed = jax.random.permutation(partition_keys[3], changed)[:TOP_KEY_BLOCKS]
        from_rest = jax.random.permutation(partition_keys[4], unchanged)[:TOP_KEY_BLOCKS]
        slots = jnp.arange(TOP_KEY_BLOCKS, dtype=jnp.int32)
        merged = jnp.where(slots < total_count, from_changed, from_rest)
        return jax.random.permutation(partition_keys[5], merged)
    return jax.vmap(one_row)(row_keys).astype(jnp.int32)


def steps_of(own_key, extent, shards, low, top_value):
    def one(axis_at, blocks):
        steps = jax.random.uniform(jax.random.fold_in(jax.random.fold_in(own_key, 6), axis_at), (blocks,), jnp.float32, low / len(shards), top_value / len(shards))
        return jnp.repeat(jnp.exp(steps), extent[axis_at] // blocks).reshape((-1,) + (1,) * (len(extent) - axis_at - 1))

    level = one(*shards[0])
    for cut in shards[1:]:
        level = level * one(*cut)
    return level


def scatter_about(stream_key, shape, deviation, limit, pieces=(), kind=jnp.bfloat16):
    values = jax.random.normal(stream_key, shape, jnp.float32) * deviation
    if len(pieces) > 0:
        values = steps_of(stream_key, shape, pieces, -0.22, 0.18) * values
    return jnp.clip(values, min=-limit, max=limit).astype(kind)


def setup_inputs(seed: int = 0) -> dict:
    seeds = jax.random.split(jax.random.key(seed), 7)
    return {
        "cached_probs": draw_cached_probs(jax.random.fold_in(seeds[6], 71), 0),
        "out_old": scatter_about(seeds[1], (TOKENS, HQ * HD), 1.0, 6.0, ((0, 8), (1, 4))),
        "key_lists": draw_key_lists(jax.random.fold_in(seeds[6], 71), 0),
        "changed_block_numbers": draw_changed_block_numbers(jax.random.fold_in(seeds[6], 71), 0),
        "delta_v": scatter_about(seeds[4], (NCB * BLK, KVH * HD), 4.0, 24.0, ((0, 8), (1, 4))),
        "w_out": scatter_about(seeds[5], (HQ * HD, D), (HQ * HD) ** -0.5, 0.078125, ((0, 4), (1, 8))),
    }


def reference(cached_probs, out_old, key_lists, changed_block_numbers, delta_v, w_out):
    changes_f = delta_v.reshape(NCB, BLK * KVH * HD).astype(jnp.float32)

    def one_block(inputs):
        prob_tiles, block_listing = inputs
        onehot = (block_listing[:, None] == changed_block_numbers[None, :]).astype(jnp.float32)
        picked = jnp.dot(onehot, changes_f).astype(jnp.bfloat16)
        picked = picked.reshape(TOP_KEY_BLOCKS, BLK, KVH, HD).astype(jnp.float32)
        weights = prob_tiles.astype(jnp.float32).reshape(KVH, GROUP, TOP_KEY_BLOCKS, BLK, BLK)
        result = jnp.einsum("vgkij,kjvd->ivgd", weights, picked)
        return result.reshape(BLK, HQ * HD)

    delta_out = lax.map(one_block, (cached_probs, key_lists)).reshape(TOKENS, HQ * HD)
    attn_new = (out_old.astype(jnp.float32) + delta_out).astype(jnp.bfloat16)
    width = HQ_DEV * HD
    summed = jnp.zeros((TOKENS, D), jnp.float32)
    for group in range(N_HEAD):
        partial_value = jnp.dot(attn_new[:, group * width:(group + 1) * width], w_out[group * width:(group + 1) * width, :], preferred_element_type=jnp.float32).astype(jnp.bfloat16)
        partial_value = lax.optimization_barrier(partial_value)
        summed = summed + partial_value.astype(jnp.float32)
    return attn_new, summed.astype(jnp.bfloat16)
```

```python
import functools

import jax
import jax.numpy as jnp
from jax import lax
from jax.experimental import pallas as pl
from jax.experimental.pallas import tpu as pltpu
from jax.sharding import PartitionSpec as P

BLK = 128
GROUP = 5
BOTH = ("seq", "head")
MIB = 1 << 20


def attention_kernel(slot_ref, probs_ref, old_ref, near_ref, far_ref, new_ref, held, total, arrived):
    blocks, heads, topk = probs_ref.shape[:3]
    values = heads // GROUP

    def copy(q, k):
        at = q * topk + k
        return pltpu.make_async_copy(probs_ref.at[q, :, k], held.at[at], arrived.at[at])

    for q in range(blocks):
        for k in range(topk):

            @pl.when(slot_ref[q * topk + k] >= 0)
            def _():
                copy(q, k).start()

    total[...] = old_ref[...].astype(jnp.float32)

    @pl.loop(0, blocks)
    def _(q):
        rows = pl.ds(pl.multiple_of(q * BLK, BLK), BLK)

        @pl.loop(0, topk)
        def _(k):
            slot = slot_ref[q * topk + k]

            @pl.when(slot >= 0)
            def _():
                copy(q, k).wait()
                place = lax.shift_right_logical(slot, 1)
                change = jnp.where(lax.bitwise_and(slot, 1) == 1, far_ref[place], near_ref[place])
                for v in range(values):
                    weights = held[q * topk + k, v * GROUP:(v + 1) * GROUP].reshape(GROUP * BLK, BLK)
                    part = jnp.dot(weights, change[:, v * BLK:(v + 1) * BLK], preferred_element_type=jnp.float32)
                    for g in range(GROUP):
                        at = (v * GROUP + g) * BLK
                        total[rows, at:at + BLK] += part[g * BLK:(g + 1) * BLK]

    new_ref[...] = total[...].astype(jnp.bfloat16)


def refresh(slots, cached_probs, out_old, near, far):
    blocks, heads, topk = cached_probs.shape[:3]
    near = near.reshape(-1, BLK, near.shape[-1])
    far = far.reshape(-1, BLK, far.shape[-1])
    flops = 2 * cached_probs.size * BLK // 4
    return pl.pallas_call(
        attention_kernel,
        out_shape=jax.ShapeDtypeStruct(out_old.shape, jnp.bfloat16),
        grid_spec=pltpu.PrefetchScalarGridSpec(
            num_scalar_prefetch=1,
            grid=(),
            in_specs=[pl.BlockSpec(memory_space=pl.ANY)] + [pl.BlockSpec(memory_space=pltpu.VMEM)] * 3,
            out_specs=pl.BlockSpec(memory_space=pltpu.VMEM),
            scratch_shapes=[
                pltpu.VMEM((blocks * topk, heads, BLK, BLK), jnp.bfloat16),
                pltpu.VMEM(out_old.shape, jnp.float32),
                pltpu.SemaphoreType.DMA((blocks * topk,)),
            ],
        ),
        compiler_params=pltpu.CompilerParams(vmem_limit_bytes=32 * MIB),
        cost_estimate=pl.CostEstimate(flops=flops, bytes_accessed=cached_probs.size, transcendentals=0),
        name="attention",
    )(slots, cached_probs, out_old, near, far)


def product_kernel(count, *refs):
    lefts, right_ref, out_ref = refs[:count], refs[count], refs[count + 1]
    base = 0
    for left in lefts:
        step = min(256, left.shape[0])

        @pl.loop(0, left.shape[0] // step)
        def _(i, left=left, base=base, step=step):
            at = pl.multiple_of(i * step, step)
            out_ref[pl.ds(base + at, step), :] = jnp.dot(
                left[pl.ds(at, step), :], right_ref[...], preferred_element_type=jnp.float32
            ).astype(jnp.bfloat16)

        base += left.shape[0]


def product(lefts, right):
    rows, depth, width = sum(left.shape[0] for left in lefts), right.shape[0], right.shape[1]
    return pl.pallas_call(
        functools.partial(product_kernel, len(lefts)),
        out_shape=jax.ShapeDtypeStruct((rows, width), jnp.bfloat16),
        in_specs=[pl.BlockSpec(memory_space=pltpu.VMEM)] * (len(lefts) + 1),
        out_specs=pl.BlockSpec(memory_space=pltpu.VMEM),
        compiler_params=pltpu.CompilerParams(vmem_limit_bytes=32 * MIB),
        cost_estimate=pl.CostEstimate(
            flops=2 * rows * depth * width,
            bytes_accessed=2 * (rows * depth + depth * width + rows * width),
            transcendentals=0,
        ),
        name="product",
    )(*lefts, right)


def add(a, b):
    return (a.astype(jnp.float32) + b.astype(jnp.float32)).astype(jnp.bfloat16)


def slots_of(key_lists, changed_block_numbers, me):
    count = changed_block_numbers.shape[0]
    places = jnp.bitwise_xor(jnp.arange(count, dtype=jnp.int32), me)
    hit = key_lists.reshape(-1)[:, None] == changed_block_numbers[None, :]
    return jnp.max(jnp.where(hit, places[None, :], -1), axis=1)


def local_any(cached_probs, out_old, key_lists, changed_block_numbers, delta_v, w_out):
    every = lax.all_gather(delta_v, "seq", axis=0, tiled=True)
    every = every.reshape(-1, 2, BLK, every.shape[-1])
    slots = slots_of(key_lists, changed_block_numbers, jnp.int32(0))
    attn_new = refresh(slots, cached_probs, out_old, every[:, 0], every[:, 1])
    terms = jnp.dot(
        attn_new, lax.all_gather(w_out, "seq", axis=1, tiled=True), preferred_element_type=jnp.float32
    )
    out_proj = lax.psum_scatter(terms.astype(jnp.bfloat16), "head", scatter_dimension=1, tiled=True)
    return attn_new, out_proj


def move(value, where):
    pairs = []
    for z in range(4):
        for x in range(2):
            for y in range(2):
                for c in range(2):
                    to = where(z, x, y, c)
                    if to is not None:
                        tz, tx, ty, tc = to
                        pairs.append((((z * 2 + x) * 2 + y) * 2 + c, ((tz * 2 + tx) * 2 + ty) * 2 + tc))
    return lax.ppermute(value, BOTH, pairs)


def inner(z):
    return z in (1, 2)


CUTS = (384, 256)


def local_line(cached_probs, out_old, key_lists, changed_block_numbers, delta_v, w_out):
    s, h = lax.axis_index("seq"), lax.axis_index("head")
    z, x, y, c = s // 2, s % 2, h // 2, h % 2
    half = z // 2
    is_inner = (z == 1) | (z == 2)
    rows = out_old.shape[0]

    line = [delta_v] + [move(delta_v, lambda z, x, y, c, k=k: (z ^ k, x, y, c)) for k in (1, 2, 3)]
    near = jnp.concatenate(line, axis=0)
    far = move(near, lambda z, x, y, c: (z, 1 - x, y, c))

    pair = move(w_out, lambda z, x, y, c: (z ^ 1, x, y, c))
    cross = move(w_out, lambda z, x, y, c: (3 - z, x, y, c) if inner(z) else None)
    cross_end = move(cross, lambda z, x, y, c: (z ^ 1, x, y, c) if inner(z) else None)
    lasts, at = [], 0
    for width in CUTS:
        lasts.append(move(pair[:, at:at + width], lambda z, x, y, c: (3 - z, x, y, c) if inner(z) else None))
        at += width

    slots = slots_of(key_lists, changed_block_numbers, s.astype(jnp.int32))
    attn_new = refresh(slots, cached_probs, out_old, near, far)

    other = move(attn_new, lambda z, x, y, c: (z, 1 - x, y, c))
    ends = [
        move(attn_new[r:r + rows // 2], lambda z, x, y, c: None if inner(z) else (z ^ 1, x, y, c))
        for r in (0, rows // 2)
    ]
    ends_other = [move(v, lambda z, x, y, c: (z, 1 - x, y, c) if inner(z) else None) for v in ends]

    mine = [attn_new, other]
    p_own, p_pair = product(mine, w_out), product(mine, pair)
    keep = z % 2 == c
    s_half = add(
        jnp.where(keep, p_own, p_pair),
        move(jnp.where(keep, p_pair, p_own), lambda z, x, y, c: (z, x, y, 1 - c)),
    )
    p_cross = product(mine, jnp.where(is_inner, cross, cross_end))
    s_cross = add(p_cross, move(p_cross, lambda z, x, y, c: (z, x, y, 1 - c) if c != z // 2 else None))
    over = move(
        jnp.where(y == half, s_cross, s_half),
        lambda z, x, y, c: (z, x, 1 - y, c) if y != z // 2 or c == z // 2 else None,
    )
    done = add(jnp.where(y == half, s_half, s_cross), over)
    done_far = move(
        done[rows:], lambda z, x, y, c: (z, 1 - x, y, c) if y == z // 2 or c == z // 2 else None
    )

    nears, fars = [], []
    for last in lasts:
        p = product(mine + ends + ends_other, last)
        sums = add(p, move(p, lambda z, x, y, c: (z, x, y, 1 - c) if inner(z) and c == z // 2 else None))
        full = add(
            sums,
            move(
                sums,
                lambda z, x, y, c: (z, x, 1 - y, c) if inner(z) and y == z // 2 and c != z // 2 else None,
            ),
        )

        def send(value, to):
            return move(
                value,
                lambda z, x, y, c: to(z, x, y, c) if inner(z) and y != z // 2 and c != z // 2 else None,
            )

        far_inner = send(full[rows:2 * rows], lambda z, x, y, c: (z, 1 - x, y, c))
        near_end = send(full[2 * rows:3 * rows], lambda z, x, y, c: (z ^ 1, x, y, c))
        far_end = send(full[3 * rows:], lambda z, x, y, c: (z ^ 1, 1 - x, y, c))
        nears.append(jnp.where(is_inner, full[:rows], near_end))
        fars.append(jnp.where(is_inner, far_inner, far_end))

    is_last = (y != half) & (c != half)
    near_half = jnp.where(is_last, jnp.concatenate(nears, axis=1), done[:rows])
    far_half = jnp.where(is_last, jnp.concatenate(fars, axis=1), done_far)
    first = jnp.where(x == 0, near_half, far_half)
    second = jnp.where(x == 0, far_half, near_half)
    return attn_new, jnp.concatenate([first, second], axis=1)


def solution(mesh):
    placed = (
        P("seq", "head", None, None, None),
        P("seq", "head"),
        P("seq", None),
        P(),
        P("seq", "head"),
        P("head", "seq"),
    )
    on_line = mesh.shape["seq"] == 8 and mesh.shape["head"] == 4
    return jax.shard_map(
        local_line if on_line else local_any,
        mesh=mesh,
        in_specs=placed,
        out_specs=(P("seq", "head"), P("seq", "head")),
        check_vma=False,
    )
```

```python
import functools

import jax
import jax.numpy as jnp
from jax import lax
from jax.experimental import pallas as pl
from jax.experimental.pallas import tpu as pltpu
from jax.sharding import PartitionSpec as P

BLK = 128
GROUP = 5
BOTH = ("seq", "head")
MIB = 1 << 20


def attention_kernel(slot_ref, probs_ref, old_ref, near_ref, far_ref, new_ref, held, total, old, near, far, arrived, loaded):
    blocks, heads, topk = probs_ref.shape[:3]
    values = heads // GROUP

    def copy(q, k):
        at = q * topk + k
        return pltpu.make_async_copy(probs_ref.at[q, :, k], held.at[at], arrived.at[at])

    loads = [
        pltpu.make_async_copy(source, target, loaded.at[i])
        for i, (source, target) in enumerate(((near_ref, near), (far_ref, far), (old_ref, old)))
    ]
    for load in loads:
        load.start()
    for q in range(blocks):
        for k in range(topk):

            @pl.when(slot_ref[q * topk + k] >= 0)
            def _():
                copy(q, k).start()

    for load in loads:
        load.wait()
    total[...] = old[...].astype(jnp.float32)

    @pl.loop(0, blocks)
    def _(q):
        rows = pl.ds(pl.multiple_of(q * BLK, BLK), BLK)

        @pl.loop(0, topk)
        def _(k):
            slot = slot_ref[q * topk + k]

            @pl.when(slot >= 0)
            def _():
                copy(q, k).wait()
                place = lax.shift_right_logical(slot, 1)
                change = jnp.where(lax.bitwise_and(slot, 1) == 1, far[place], near[place])
                for v in range(values):
                    weights = held[q * topk + k, v * GROUP:(v + 1) * GROUP].reshape(GROUP * BLK, BLK)
                    part = jnp.dot(weights, change[:, v * BLK:(v + 1) * BLK], preferred_element_type=jnp.float32)
                    for g in range(GROUP):
                        at = (v * GROUP + g) * BLK
                        total[rows, at:at + BLK] += part[g * BLK:(g + 1) * BLK]

    new_ref[...] = total[...].astype(jnp.bfloat16)


def refresh(slots, cached_probs, out_old, near, far):
    blocks, heads, topk = cached_probs.shape[:3]
    near = near.reshape(-1, BLK, near.shape[-1])
    far = far.reshape(-1, BLK, far.shape[-1])
    return pl.pallas_call(
        attention_kernel,
        out_shape=jax.ShapeDtypeStruct(out_old.shape, jnp.bfloat16),
        in_specs=[pl.BlockSpec(memory_space=pltpu.SMEM)] + [pl.BlockSpec(memory_space=pl.ANY)] * 4,
        out_specs=pl.BlockSpec(memory_space=pltpu.VMEM),
        scratch_shapes=[
            pltpu.VMEM((blocks * topk, heads, BLK, BLK), jnp.bfloat16),
            pltpu.VMEM(out_old.shape, jnp.float32),
            pltpu.VMEM(out_old.shape, jnp.bfloat16),
            pltpu.VMEM(near.shape, jnp.bfloat16),
            pltpu.VMEM(far.shape, jnp.bfloat16),
            pltpu.SemaphoreType.DMA((blocks * topk,)),
            pltpu.SemaphoreType.DMA((3,)),
        ],
        compiler_params=pltpu.CompilerParams(vmem_limit_bytes=56 * MIB),
        cost_estimate=pl.CostEstimate(flops=MIB, bytes_accessed=MIB, transcendentals=0),
        name="attention",
    )(slots, cached_probs, out_old, near, far)


def product_kernel(count, pick_ref, new_ref, over_ref, other_ref, *refs):
    sources, out_ref = refs[:2 * count], refs[2 * count]
    left, *rights, loaded = refs[2 * count + 1:]
    depth = new_ref.shape[1]
    halves = (slice(0, depth), slice(depth, 2 * depth))

    def load_left(i, source):
        return pltpu.make_async_copy(source, left.at[:, halves[i]], loaded.at[i])

    load_left(1, other_ref).start()

    @pl.when(pick_ref[0] == 1)
    def _():
        load_left(0, new_ref).start()

    @pl.when(pick_ref[0] == 0)
    def _():
        load_left(0, over_ref).start()

    loads = [
        pltpu.make_async_copy(sources[i], rights[i // 2].at[halves[i % 2], :], loaded.at[2 + i])
        for i in range(2 * count)
    ]
    for load in loads:
        load.start()
    load_left(0, over_ref).wait()
    load_left(1, other_ref).wait()
    column = 0
    for j in range(count):
        width = rights[j].shape[1]
        loads[2 * j].wait()
        loads[2 * j + 1].wait()
        out_ref[:, column:column + width] = jnp.dot(
            left[...], rights[j][...], preferred_element_type=jnp.float32
        ).astype(jnp.bfloat16)
        column += width


def product(pick, lefts, rights):
    rows, depth = lefts[0].shape
    width = sum(same.shape[1] for same, _ in rights)
    flat = [block for pair in rights for block in pair]
    return pl.pallas_call(
        functools.partial(product_kernel, len(rights)),
        out_shape=jax.ShapeDtypeStruct((rows, width), jnp.bfloat16),
        in_specs=[pl.BlockSpec(memory_space=pltpu.SMEM)]
        + [pl.BlockSpec(memory_space=pl.ANY)] * (len(lefts) + len(flat)),
        out_specs=pl.BlockSpec(memory_space=pltpu.VMEM),
        scratch_shapes=[pltpu.VMEM((rows, 2 * depth), jnp.bfloat16)]
        + [pltpu.VMEM((2 * depth, block.shape[1]), jnp.bfloat16) for block, _ in rights]
        + [pltpu.SemaphoreType.DMA((2 + len(flat),))],
        compiler_params=pltpu.CompilerParams(vmem_limit_bytes=56 * MIB),
        cost_estimate=pl.CostEstimate(flops=MIB, bytes_accessed=MIB, transcendentals=0),
        name="product",
    )(pick, *lefts, *flat)


def add(a, b):
    return (a.astype(jnp.float32) + b.astype(jnp.float32)).astype(jnp.bfloat16)


def slots_of(key_lists, changed_block_numbers, me):
    count = changed_block_numbers.shape[0]
    places = jnp.bitwise_xor(jnp.arange(count, dtype=jnp.int32), me)
    hit = key_lists.reshape(-1)[:, None] == changed_block_numbers[None, :]
    return jnp.max(jnp.where(hit, places[None, :], -1), axis=1)


def local_any(cached_probs, out_old, key_lists, changed_block_numbers, delta_v, w_out):
    every = lax.all_gather(delta_v, "seq", axis=0, tiled=True)
    every = every.reshape(-1, 2, BLK, every.shape[-1])
    slots = slots_of(key_lists, changed_block_numbers, jnp.int32(0))
    attn_new = refresh(slots, cached_probs, out_old, every[:, 0], every[:, 1])
    terms = jnp.dot(
        attn_new, lax.all_gather(w_out, "seq", axis=1, tiled=True), preferred_element_type=jnp.float32
    )
    out_proj = lax.psum_scatter(terms.astype(jnp.bfloat16), "head", scatter_dimension=1, tiled=True)
    return attn_new, out_proj


def move(value, where):
    pairs = []
    for z in range(4):
        for x in range(2):
            for y in range(2):
                for c in range(2):
                    to = where(z, x, y, c)
                    if to is not None:
                        tz, tx, ty, tc = to
                        pairs.append((((z * 2 + x) * 2 + y) * 2 + c, ((tz * 2 + tx) * 2 + ty) * 2 + tc))
    return lax.ppermute(value, BOTH, pairs)


def inner(z):
    return z in (1, 2)


CUTS = (384, 256)


def columns(value, cuts=CUTS):
    at, parts = 0, []
    for width in cuts:
        parts.append(value[:, at:at + width])
        at += width
    return parts


def tie(*values):
    return lax.optimization_barrier(values)


def local_line(cached_probs, out_old, key_lists, changed_block_numbers, delta_v, w_out):
    s, h = lax.axis_index("seq"), lax.axis_index("head")
    z, x, y, c = s // 2, s % 2, h // 2, h % 2
    half = z // 2
    is_inner = (z == 1) | (z == 2)

    def to_core(value):
        return move(value, lambda z, x, y, c: (z, x, y, 1 - c))

    def to_pair(value):
        return move(value, lambda z, x, y, c: (z ^ 1, x, y, c))

    def to_cross(value):
        return move(value, lambda z, x, y, c: (3 - z, x, y, c) if inner(z) else (z, x, y, 1 - c))

    def to_far_end(value):
        return move(value, lambda z, x, y, c: (z ^ 2 if inner(z) else z ^ 1, x, y, c))

    line = [move(delta_v, lambda z, x, y, c, k=k: (z ^ k, x, y, c)) for k in (1, 2, 3)]
    w_out, line = tie(w_out, line)
    near = jnp.concatenate([delta_v] + line, axis=0)
    far = move(near, lambda z, x, y, c: (z, 1 - x, y, c))
    pair, cross = to_pair(w_out), to_cross(w_out)
    cross_end = to_pair(cross)
    last = to_cross(pair)

    slots = slots_of(key_lists, changed_block_numbers, s.astype(jnp.int32))
    attn_new = refresh(slots, cached_probs, out_old, near, far)
    over_x = move(attn_new, lambda z, x, y, c: (z, 1 - x, y, c))
    other = to_core(jnp.where(x == c, over_x, attn_new))
    pick = (x == c).astype(jnp.int32).reshape(1)
    rows = [attn_new, over_x, other]

    def with_other(block):
        return block, to_core(block)

    def reduced(p_half, p_cross):
        over = move(jnp.where(y == half, p_cross, p_half), lambda z, x, y, c: (z, x, 1 - y, c))
        return add(jnp.where(y == half, p_half, p_cross), over)

    p_half = product(pick, rows, [with_other(v) for v in (w_out, pair)])
    p_own, p_pair = columns(p_half, (w_out.shape[1], w_out.shape[1]))
    parts = columns(pair)
    parts[0], p_half, last, cross_end = tie(parts[0], p_half, last, cross_end)
    block = jnp.where(is_inner, cross, cross_end)
    p_cross = product(pick, rows, [with_other(v) for v in columns(block)])
    last_end = [to_far_end(parts[0])]
    parts[1], p_cross = tie(parts[1], p_cross)
    last_end.append(to_far_end(parts[1]))
    last_end[0], p_cross = tie(last_end[0], p_cross)
    first = columns(reduced(p_own, p_cross))
    second = []
    for p_pair, inner_part, end_part in zip(columns(p_pair), columns(last), last_end, strict=True):
        if second:
            p_last, end_part = tie(p_last, end_part)
        p_last = product(pick, rows, [with_other(jnp.where(is_inner, inner_part, end_part))])
        second.append(reduced(p_pair, p_last))

    first_core = jnp.where(y == half, z % 2, half)
    out = []
    for mine, other in zip(first, second, strict=True):
        for_core = [jnp.where(first_core == j, mine, other) for j in (0, 1)]
        by_same = move(
            jnp.where(x == 0, for_core[0], for_core[1]),
            lambda z, x, y, c: (z, x, 1 - y, c) if x == c else (z, c, y, x),
        )
        by_other = move(
            jnp.where(x == 0, for_core[1], for_core[0]), lambda z, x, y, c: (z, c, y, 1 - x)
        )
        stays = jnp.where(c == 0, for_core[0], for_core[1])
        out.append((jnp.where(x == c, stays, by_same), by_other))
    left = jnp.concatenate([jnp.where(c == 0, a, b) for a, b in out], axis=1)
    right = jnp.concatenate([jnp.where(c == 0, b, a) for a, b in out], axis=1)
    return attn_new, jnp.concatenate([left, right], axis=1)


def solution(mesh):
    placed = (
        P("seq", "head", None, None, None),
        P("seq", "head"),
        P("seq", None),
        P(),
        P("seq", "head"),
        P("head", "seq"),
    )
    on_line = mesh.shape["seq"] == 8 and mesh.shape["head"] == 4
    return jax.shard_map(
        local_line if on_line else local_any,
        mesh=mesh,
        in_specs=placed,
        out_specs=(P("seq", "head"), P("seq", "head")),
        check_vma=False,
    )
```

```python
import functools

import jax
import jax.numpy as jnp
from jax import lax
from jax.experimental import pallas as pl
from jax.experimental.pallas import tpu as pltpu
from jax.sharding import PartitionSpec as P

BLK = 128
GROUP = 5
BOTH = ("seq", "head")
MIB = 1 << 20


def attention_kernel(slot_ref, probs_ref, old_ref, near_ref, far_ref, new_ref, held, total, old, near, far, arrived, loaded):
    blocks, heads, topk = probs_ref.shape[:3]
    values = heads // GROUP

    def copy(q, k):
        at = q * topk + k
        return pltpu.make_async_copy(probs_ref.at[q, :, k], held.at[at], arrived.at[at])

    loads = [
        pltpu.make_async_copy(source, target, loaded.at[i])
        for i, (source, target) in enumerate(((near_ref, near), (far_ref, far), (old_ref, old)))
    ]
    for load in loads:
        load.start()
    for q in range(blocks):
        for k in range(topk):

            @pl.when(slot_ref[q * topk + k] >= 0)
            def _():
                copy(q, k).start()

    for load in loads:
        load.wait()
    total[...] = old[...].astype(jnp.float32)

    @pl.loop(0, blocks)
    def _(q):
        rows = pl.ds(pl.multiple_of(q * BLK, BLK), BLK)

        @pl.loop(0, topk)
        def _(k):
            slot = slot_ref[q * topk + k]

            @pl.when(slot >= 0)
            def _():
                copy(q, k).wait()
                place = lax.shift_right_logical(slot, 1)
                change = jnp.where(lax.bitwise_and(slot, 1) == 1, far[place], near[place])
                for v in range(values):
                    weights = held[q * topk + k, v * GROUP:(v + 1) * GROUP].reshape(GROUP * BLK, BLK)
                    part = jnp.dot(weights, change[:, v * BLK:(v + 1) * BLK], preferred_element_type=jnp.float32)
                    for g in range(GROUP):
                        at = (v * GROUP + g) * BLK
                        total[rows, at:at + BLK] += part[g * BLK:(g + 1) * BLK]

    new_ref[...] = total[...].astype(jnp.bfloat16)


def refresh(slots, cached_probs, out_old, near, far):
    blocks, heads, topk = cached_probs.shape[:3]
    near = near.reshape(-1, BLK, near.shape[-1])
    far = far.reshape(-1, BLK, far.shape[-1])
    return pl.pallas_call(
        attention_kernel,
        out_shape=jax.ShapeDtypeStruct(out_old.shape, jnp.bfloat16),
        in_specs=[pl.BlockSpec(memory_space=pltpu.SMEM)] + [pl.BlockSpec(memory_space=pl.ANY)] * 4,
        out_specs=pl.BlockSpec(memory_space=pltpu.VMEM),
        scratch_shapes=[
            pltpu.VMEM((blocks * topk, heads, BLK, BLK), jnp.bfloat16),
            pltpu.VMEM(out_old.shape, jnp.float32),
            pltpu.VMEM(out_old.shape, jnp.bfloat16),
            pltpu.VMEM(near.shape, jnp.bfloat16),
            pltpu.VMEM(far.shape, jnp.bfloat16),
            pltpu.SemaphoreType.DMA((blocks * topk,)),
            pltpu.SemaphoreType.DMA((3,)),
        ],
        compiler_params=pltpu.CompilerParams(vmem_limit_bytes=56 * MIB),
        cost_estimate=pl.CostEstimate(flops=MIB, bytes_accessed=MIB, transcendentals=0),
        name="attention",
    )(slots, cached_probs, out_old, near, far)


def product_kernel(count, pick_ref, new_ref, over_ref, other_ref, *refs):
    sources, out_ref, left, right, loaded = refs[:2 * count], *refs[2 * count:]
    depth = new_ref.shape[1]
    halves = (slice(0, depth), slice(depth, 2 * depth))

    def load_left(i, source):
        return pltpu.make_async_copy(source, left.at[:, halves[i]], loaded.at[i])

    load_left(1, other_ref).start()

    @pl.when(pick_ref[0] == 1)
    def _():
        load_left(0, new_ref).start()

    @pl.when(pick_ref[0] == 0)
    def _():
        load_left(0, over_ref).start()

    loads, column = [], 0
    for j in range(count):
        width = sources[2 * j].shape[1]
        for i in (0, 1):
            target = right.at[halves[i], column:column + width]
            loads.append(pltpu.make_async_copy(sources[2 * j + i], target, loaded.at[2 + 2 * j + i]))
            loads[-1].start()
        column += width
    load_left(0, over_ref).wait()
    load_left(1, other_ref).wait()
    for load in loads:
        load.wait()
    out_ref[...] = jnp.dot(left[...], right[...], preferred_element_type=jnp.float32).astype(jnp.bfloat16)


def product(pick, lefts, rights):
    rows, depth = lefts[0].shape
    width = sum(same.shape[1] for same, _ in rights)
    flat = [block for pair in rights for block in pair]
    return pl.pallas_call(
        functools.partial(product_kernel, len(rights)),
        out_shape=jax.ShapeDtypeStruct((rows, width), jnp.bfloat16),
        in_specs=[pl.BlockSpec(memory_space=pltpu.SMEM)]
        + [pl.BlockSpec(memory_space=pl.ANY)] * (len(lefts) + len(flat)),
        out_specs=pl.BlockSpec(memory_space=pltpu.VMEM),
        scratch_shapes=[
            pltpu.VMEM((rows, 2 * depth), jnp.bfloat16),
            pltpu.VMEM((2 * depth, width), jnp.bfloat16),
            pltpu.SemaphoreType.DMA((2 + len(flat),)),
        ],
        compiler_params=pltpu.CompilerParams(vmem_limit_bytes=56 * MIB),
        cost_estimate=pl.CostEstimate(flops=MIB, bytes_accessed=MIB, transcendentals=0),
        name="product",
    )(pick, *lefts, *flat)


def add(a, b):
    return (a.astype(jnp.float32) + b.astype(jnp.float32)).astype(jnp.bfloat16)


def slots_of(key_lists, changed_block_numbers, me):
    count = changed_block_numbers.shape[0]
    places = jnp.bitwise_xor(jnp.arange(count, dtype=jnp.int32), me)
    hit = key_lists.reshape(-1)[:, None] == changed_block_numbers[None, :]
    return jnp.max(jnp.where(hit, places[None, :], -1), axis=1)


def local_any(cached_probs, out_old, key_lists, changed_block_numbers, delta_v, w_out):
    every = lax.all_gather(delta_v, "seq", axis=0, tiled=True)
    every = every.reshape(-1, 2, BLK, every.shape[-1])
    slots = slots_of(key_lists, changed_block_numbers, jnp.int32(0))
    attn_new = refresh(slots, cached_probs, out_old, every[:, 0], every[:, 1])
    terms = jnp.dot(
        attn_new, lax.all_gather(w_out, "seq", axis=1, tiled=True), preferred_element_type=jnp.float32
    )
    out_proj = lax.psum_scatter(terms.astype(jnp.bfloat16), "head", scatter_dimension=1, tiled=True)
    return attn_new, out_proj


def move(value, where):
    pairs = []
    for z in range(4):
        for x in range(2):
            for y in range(2):
                for c in range(2):
                    to = where(z, x, y, c)
                    if to is not None:
                        tz, tx, ty, tc = to
                        pairs.append((((z * 2 + x) * 2 + y) * 2 + c, ((tz * 2 + tx) * 2 + ty) * 2 + tc))
    return lax.ppermute(value, BOTH, pairs)


def inner(z):
    return z in (1, 2)


CUTS = (384, 256)


def columns(value, cuts=CUTS):
    at, parts = 0, []
    for width in cuts:
        parts.append(value[:, at:at + width])
        at += width
    return parts


def narrow(value):
    return columns(value, [BLK] * (value.shape[1] // BLK))


def tie(*values):
    return lax.optimization_barrier(values)


def local_line(cached_probs, out_old, key_lists, changed_block_numbers, delta_v, w_out):
    s, h = lax.axis_index("seq"), lax.axis_index("head")
    z, x, y, c = s // 2, s % 2, h // 2, h % 2
    half = z // 2
    is_inner = (z == 1) | (z == 2)

    def to_core(value):
        return move(value, lambda z, x, y, c: (z, x, y, 1 - c))

    def to_pair(value):
        return move(value, lambda z, x, y, c: (z ^ 1, x, y, c))

    def to_cross(value):
        return move(value, lambda z, x, y, c: (3 - z, x, y, c) if inner(z) else (z, x, y, 1 - c))

    def to_far_end(value):
        return move(value, lambda z, x, y, c: (z ^ 2 if inner(z) else z ^ 1, x, y, c))

    line = [move(delta_v, lambda z, x, y, c, k=k: (z ^ k, x, y, c)) for k in (1, 2, 3)]
    near = jnp.concatenate([delta_v] + line, axis=0)
    far = move(near, lambda z, x, y, c: (z, 1 - x, y, c))
    pair, cross = to_pair(w_out), to_cross(w_out)
    cross_end = to_pair(cross)
    last = to_cross(pair)

    slots = slots_of(key_lists, changed_block_numbers, s.astype(jnp.int32))
    attn_new = refresh(slots, cached_probs, out_old, near, far)
    over_x = move(attn_new, lambda z, x, y, c: (z, 1 - x, y, c))
    other = to_core(jnp.where(x == c, over_x, attn_new))
    pick = (x == c).astype(jnp.int32).reshape(1)
    rows = [attn_new, over_x, other]

    def with_other(block):
        return block, to_core(block)

    def to_sum(p_half, p_cross):
        return jnp.where(y == half, p_cross, p_half), jnp.where(y == half, p_half, p_cross)

    def summed(sent, kept):
        return add(kept, move(sent, lambda z, x, y, c: (z, x, 1 - y, c)))

    p_half = product(pick, rows, [with_other(v) for v in (w_out, pair)])
    p_own, p_pair = columns(p_half, (w_out.shape[1], w_out.shape[1]))
    parts = columns(pair)
    parts[0], p_half, last, cross_end = tie(parts[0], p_half, last, cross_end)
    block = jnp.where(is_inner, cross, cross_end)
    p_cross = product(pick, rows, [with_other(v) for v in columns(block)])
    last_end = [to_far_end(parts[0])]
    parts[1], block = tie(parts[1], block)
    last_end.append(to_far_end(parts[1]))
    first = summed(*to_sum(p_own, p_cross))
    last_end[0], first = tie(last_end[0], first)
    first = columns(first)
    second, terms = [], None
    for p_pair, inner_part, end_part in zip(columns(p_pair), columns(last), last_end, strict=True):
        if terms:
            *terms, end_part = tie(*terms, end_part)
            second.append(summed(*terms))
        pieces = [jnp.where(is_inner, *v) for v in zip(narrow(inner_part), narrow(end_part), strict=True)]
        p_last = product(pick, rows, [with_other(v) for v in pieces])
        terms = to_sum(p_pair, p_last)
    second.append(summed(*terms))

    first_core = jnp.where(y == half, z % 2, half)
    out = []
    for mine, other in zip(first, second, strict=True):
        for_core = [jnp.where(first_core == j, mine, other) for j in (0, 1)]
        by_same = move(
            jnp.where(x == 0, for_core[0], for_core[1]),
            lambda z, x, y, c: (z, x, 1 - y, c) if x == c else (z, c, y, x),
        )
        by_other = move(
            jnp.where(x == 0, for_core[1], for_core[0]), lambda z, x, y, c: (z, c, y, 1 - x)
        )
        stays = jnp.where(c == 0, for_core[0], for_core[1])
        out.append((jnp.where(x == c, stays, by_same), by_other))
    left = jnp.concatenate([jnp.where(c == 0, a, b) for a, b in out], axis=1)
    right = jnp.concatenate([jnp.where(c == 0, b, a) for a, b in out], axis=1)
    return attn_new, jnp.concatenate([left, right], axis=1)


def solution(mesh):
    placed = (
        P("seq", "head", None, None, None),
        P("seq", "head"),
        P("seq", None),
        P(),
        P("seq", "head"),
        P("head", "seq"),
    )
    on_line = mesh.shape["seq"] == 8 and mesh.shape["head"] == 4
    return jax.shard_map(
        local_line if on_line else local_any,
        mesh=mesh,
        in_specs=placed,
        out_specs=(P("seq", "head"), P("seq", "head")),
        check_vma=False,
    )
```

```python
import functools

import jax
import jax.numpy as jnp
from jax import lax
from jax.experimental import pallas as pl
from jax.experimental.pallas import tpu as pltpu
from jax.sharding import PartitionSpec as P

BLK = 128
GROUP = 5
BOTH = ("seq", "head")
MIB = 1 << 20


def attention_kernel(slot_ref, probs_ref, old_ref, near_ref, far_ref, new_ref, held, total, old, near, far, arrived, loaded):
    blocks, heads, topk = probs_ref.shape[:3]
    values = heads // GROUP

    def copy(q, k):
        at = q * topk + k
        return pltpu.make_async_copy(probs_ref.at[q, :, k], held.at[at], arrived.at[at])

    loads = [
        pltpu.make_async_copy(source, target, loaded.at[i])
        for i, (source, target) in enumerate(((near_ref, near), (far_ref, far), (old_ref, old)))
    ]
    for load in loads:
        load.start()
    for q in range(blocks):
        for k in range(topk):

            @pl.when(slot_ref[q * topk + k] >= 0)
            def _():
                copy(q, k).start()

    for load in loads:
        load.wait()
    total[...] = old[...].astype(jnp.float32)

    @pl.loop(0, blocks)
    def _(q):
        rows = pl.ds(pl.multiple_of(q * BLK, BLK), BLK)

        @pl.loop(0, topk)
        def _(k):
            slot = slot_ref[q * topk + k]

            @pl.when(slot >= 0)
            def _():
                copy(q, k).wait()
                place = lax.shift_right_logical(slot, 1)
                change = jnp.where(lax.bitwise_and(slot, 1) == 1, far[place], near[place])
                for v in range(values):
                    weights = held[q * topk + k, v * GROUP:(v + 1) * GROUP].reshape(GROUP * BLK, BLK)
                    part = jnp.dot(weights, change[:, v * BLK:(v + 1) * BLK], preferred_element_type=jnp.float32)
                    for g in range(GROUP):
                        at = (v * GROUP + g) * BLK
                        total[rows, at:at + BLK] += part[g * BLK:(g + 1) * BLK]

    new_ref[...] = total[...].astype(jnp.bfloat16)


def refresh(slots, cached_probs, out_old, near, far):
    blocks, heads, topk = cached_probs.shape[:3]
    near = near.reshape(-1, BLK, near.shape[-1])
    far = far.reshape(-1, BLK, far.shape[-1])
    return pl.pallas_call(
        attention_kernel,
        out_shape=jax.ShapeDtypeStruct(out_old.shape, jnp.bfloat16),
        in_specs=[pl.BlockSpec(memory_space=pltpu.SMEM)] + [pl.BlockSpec(memory_space=pl.ANY)] * 4,
        out_specs=pl.BlockSpec(memory_space=pltpu.VMEM),
        scratch_shapes=[
            pltpu.VMEM((blocks * topk, heads, BLK, BLK), jnp.bfloat16),
            pltpu.VMEM(out_old.shape, jnp.float32),
            pltpu.VMEM(out_old.shape, jnp.bfloat16),
            pltpu.VMEM(near.shape, jnp.bfloat16),
            pltpu.VMEM(far.shape, jnp.bfloat16),
            pltpu.SemaphoreType.DMA((blocks * topk,)),
            pltpu.SemaphoreType.DMA((3,)),
        ],
        compiler_params=pltpu.CompilerParams(vmem_limit_bytes=56 * MIB),
        cost_estimate=pl.CostEstimate(flops=MIB, bytes_accessed=MIB, transcendentals=0),
        name="attention",
    )(slots, cached_probs, out_old, near, far)


def product_kernel(count, pick_ref, new_ref, over_ref, other_ref, *refs):
    sources, out_ref, left, right, loaded = refs[:2 * count], *refs[2 * count:]
    depth = new_ref.shape[1]
    halves = (slice(0, depth), slice(depth, 2 * depth))

    def load_left(i, source):
        return pltpu.make_async_copy(source, left.at[:, halves[i]], loaded.at[i])

    load_left(1, other_ref).start()

    @pl.when(pick_ref[0] == 1)
    def _():
        load_left(0, new_ref).start()

    @pl.when(pick_ref[0] == 0)
    def _():
        load_left(0, over_ref).start()

    loads, column = [], 0
    for j in range(count):
        width = sources[2 * j].shape[1]
        for i in (0, 1):
            target = right.at[halves[i], column:column + width]
            loads.append(pltpu.make_async_copy(sources[2 * j + i], target, loaded.at[2 + 2 * j + i]))
            loads[-1].start()
        column += width
    load_left(0, over_ref).wait()
    load_left(1, other_ref).wait()
    for load in loads:
        load.wait()
    out_ref[...] = jnp.dot(left[...], right[...], preferred_element_type=jnp.float32).astype(jnp.bfloat16)


def product(pick, lefts, rights):
    rows, depth = lefts[0].shape
    width = sum(same.shape[1] for same, _ in rights)
    flat = [block for pair in rights for block in pair]
    return pl.pallas_call(
        functools.partial(product_kernel, len(rights)),
        out_shape=jax.ShapeDtypeStruct((rows, width), jnp.bfloat16),
        in_specs=[pl.BlockSpec(memory_space=pltpu.SMEM)]
        + [pl.BlockSpec(memory_space=pl.ANY)] * (len(lefts) + len(flat)),
        out_specs=pl.BlockSpec(memory_space=pltpu.VMEM),
        scratch_shapes=[
            pltpu.VMEM((rows, 2 * depth), jnp.bfloat16),
            pltpu.VMEM((2 * depth, width), jnp.bfloat16),
            pltpu.SemaphoreType.DMA((2 + len(flat),)),
        ],
        compiler_params=pltpu.CompilerParams(vmem_limit_bytes=56 * MIB),
        cost_estimate=pl.CostEstimate(flops=MIB, bytes_accessed=MIB, transcendentals=0),
        name="product",
    )(pick, *lefts, *flat)


def split_product_kernel(column, flag_ref, new_ref, over_ref, inner_ref, end_ref, keep_ref, *refs):
    *pass_refs, left, right, loaded = refs
    width = end_ref.shape[1]

    def load_left(i, source):
        return pltpu.make_async_copy(source, left.at[i], loaded.at[i])

    def load_right(source):
        return pltpu.make_async_copy(source, right, loaded.at[2])

    @pl.when(flag_ref[0] == 1)
    def _():
        load_left(0, new_ref).start()
        load_left(1, over_ref).start()

    @pl.when(flag_ref[0] == 0)
    def _():
        load_left(0, over_ref).start()
        load_left(1, new_ref).start()

    inner_part = inner_ref.at[:, column:column + width]

    @pl.when(flag_ref[1] == 1)
    def _():
        load_right(inner_part).start()

    @pl.when(flag_ref[1] == 0)
    def _():
        load_right(end_ref).start()

    load_right(end_ref).wait()
    load_left(1, new_ref).wait()
    passed = jnp.dot(left[1], right[...], preferred_element_type=jnp.float32).astype(jnp.bfloat16)
    for i, pass_ref in enumerate(pass_refs):
        pass_ref[...] = passed[:, i * BLK:(i + 1) * BLK]
    load_left(0, new_ref).wait()
    keep_ref[...] = jnp.dot(left[0], right[...], preferred_element_type=jnp.float32).astype(jnp.bfloat16)


def split_product(flags, lefts, inner_block, end_block, column):
    rows, depth = lefts[0].shape
    width = end_block.shape[1]
    return pl.pallas_call(
        functools.partial(split_product_kernel, column),
        out_shape=[jax.ShapeDtypeStruct((rows, width), jnp.bfloat16)]
        + [jax.ShapeDtypeStruct((rows, BLK), jnp.bfloat16)] * (width // BLK),
        in_specs=[pl.BlockSpec(memory_space=pltpu.SMEM)] + [pl.BlockSpec(memory_space=pl.ANY)] * 4,
        out_specs=[pl.BlockSpec(memory_space=pltpu.VMEM)] * (1 + width // BLK),
        scratch_shapes=[
            pltpu.VMEM((2, rows, depth), jnp.bfloat16),
            pltpu.VMEM((depth, width), jnp.bfloat16),
            pltpu.SemaphoreType.DMA((3,)),
        ],
        compiler_params=pltpu.CompilerParams(vmem_limit_bytes=56 * MIB),
        cost_estimate=pl.CostEstimate(flops=MIB, bytes_accessed=MIB, transcendentals=0),
        name="split_product",
    )(flags, *lefts, inner_block, end_block)


def add(a, b):
    return (a.astype(jnp.float32) + b.astype(jnp.float32)).astype(jnp.bfloat16)


def slots_of(key_lists, changed_block_numbers, me):
    count = changed_block_numbers.shape[0]
    places = jnp.bitwise_xor(jnp.arange(count, dtype=jnp.int32), me)
    hit = key_lists.reshape(-1)[:, None] == changed_block_numbers[None, :]
    return jnp.max(jnp.where(hit, places[None, :], -1), axis=1)


def local_any(cached_probs, out_old, key_lists, changed_block_numbers, delta_v, w_out):
    every = lax.all_gather(delta_v, "seq", axis=0, tiled=True)
    every = every.reshape(-1, 2, BLK, every.shape[-1])
    slots = slots_of(key_lists, changed_block_numbers, jnp.int32(0))
    attn_new = refresh(slots, cached_probs, out_old, every[:, 0], every[:, 1])
    terms = jnp.dot(
        attn_new, lax.all_gather(w_out, "seq", axis=1, tiled=True), preferred_element_type=jnp.float32
    )
    out_proj = lax.psum_scatter(terms.astype(jnp.bfloat16), "head", scatter_dimension=1, tiled=True)
    return attn_new, out_proj


def move(value, where):
    pairs = []
    for z in range(4):
        for x in range(2):
            for y in range(2):
                for c in range(2):
                    to = where(z, x, y, c)
                    if to is not None:
                        tz, tx, ty, tc = to
                        pairs.append((((z * 2 + x) * 2 + y) * 2 + c, ((tz * 2 + tx) * 2 + ty) * 2 + tc))
    return lax.ppermute(value, BOTH, pairs)


def inner(z):
    return z in (1, 2)


CUTS = (384, 256)


def columns(value, cuts=CUTS):
    at, parts = 0, []
    for width in cuts:
        parts.append(value[:, at:at + width])
        at += width
    return parts


def tie(*values):
    return lax.optimization_barrier(values)


def local_line(cached_probs, out_old, key_lists, changed_block_numbers, delta_v, w_out):
    s, h = lax.axis_index("seq"), lax.axis_index("head")
    z, x, y, c = s // 2, s % 2, h // 2, h % 2
    half = z // 2
    is_inner = (z == 1) | (z == 2)

    def to_core(value):
        return move(value, lambda z, x, y, c: (z, x, y, 1 - c))

    def to_pair(value):
        return move(value, lambda z, x, y, c: (z ^ 1, x, y, c))

    def to_cross(value):
        return move(value, lambda z, x, y, c: (3 - z, x, y, c) if inner(z) else (z, x, y, 1 - c))

    def to_far_end(value):
        return move(value, lambda z, x, y, c: (z ^ 2 if inner(z) else z ^ 1, x, y, c))

    line = [move(delta_v, lambda z, x, y, c, k=k: (z ^ k, x, y, c)) for k in (1, 2, 3)]
    near = jnp.concatenate([delta_v] + line, axis=0)
    far = move(near, lambda z, x, y, c: (z, 1 - x, y, c))
    pair, cross = to_pair(w_out), to_cross(w_out)
    cross_end = to_pair(cross)
    last = to_cross(pair)

    slots = slots_of(key_lists, changed_block_numbers, s.astype(jnp.int32))
    attn_new = refresh(slots, cached_probs, out_old, near, far)
    over_x = move(attn_new, lambda z, x, y, c: (z, 1 - x, y, c))
    other = to_core(jnp.where(x == c, over_x, attn_new))
    pick = (x == c).astype(jnp.int32).reshape(1)
    flags = jnp.stack([x == c, is_inner]).astype(jnp.int32)
    rows = [attn_new, over_x, other]

    def with_other(block):
        return block, to_core(block)

    def both_cores(inner_block, end_block, column):
        kept, *passed = split_product(flags, rows[:2], inner_block, end_block, column)
        return add(kept, jnp.concatenate([to_core(v) for v in passed], axis=1))

    def to_sum(p_half, p_cross):
        return jnp.where(y == half, p_cross, p_half), jnp.where(y == half, p_half, p_cross)

    def summed(sent, kept):
        return add(kept, move(sent, lambda z, x, y, c: (z, x, 1 - y, c)))

    p_half = product(pick, rows, [with_other(v) for v in (w_out, pair)])
    p_own, p_pair = columns(p_half, (w_out.shape[1], w_out.shape[1]))
    parts = columns(pair)
    parts[0], p_half, last, cross_end = tie(parts[0], p_half, last, cross_end)
    block = jnp.where(is_inner, cross, cross_end)
    p_cross = product(pick, rows, [with_other(v) for v in columns(block)])
    last_end = [to_far_end(parts[0])]
    parts[1], block = tie(parts[1], block)
    last_end.append(to_far_end(parts[1]))
    first = summed(*to_sum(p_own, p_cross))
    last_end[0], first = tie(last_end[0], first)
    first = columns(first)
    second, terms, column = [], None, 0
    for p_pair, end_part in zip(columns(p_pair), last_end, strict=True):
        if terms:
            *terms, end_part = tie(*terms, end_part)
            second.append(summed(*terms))
        p_last = both_cores(last, end_part, column)
        column += end_part.shape[1]
        if second:
            second[0], p_last = tie(second[0], p_last)
        terms = to_sum(p_pair, p_last)
    second.append(summed(*terms))

    first_core = jnp.where(y == half, z % 2, half)
    out = []
    for mine, other in zip(first, second, strict=True):
        for_core = [jnp.where(first_core == j, mine, other) for j in (0, 1)]
        by_same = move(
            jnp.where(x == 0, for_core[0], for_core[1]),
            lambda z, x, y, c: (z, x, 1 - y, c) if x == c else (z, c, y, x),
        )
        by_other = move(
            jnp.where(x == 0, for_core[1], for_core[0]), lambda z, x, y, c: (z, c, y, 1 - x)
        )
        stays = jnp.where(c == 0, for_core[0], for_core[1])
        out.append((jnp.where(x == c, stays, by_same), by_other))
    left = jnp.concatenate([jnp.where(c == 0, a, b) for a, b in out], axis=1)
    right = jnp.concatenate([jnp.where(c == 0, b, a) for a, b in out], axis=1)
    return attn_new, jnp.concatenate([left, right], axis=1)


def solution(mesh):
    placed = (
        P("seq", "head", None, None, None),
        P("seq", "head"),
        P("seq", None),
        P(),
        P("seq", "head"),
        P("head", "seq"),
    )
    on_line = mesh.shape["seq"] == 8 and mesh.shape["head"] == 4
    return jax.shard_map(
        local_line if on_line else local_any,
        mesh=mesh,
        in_specs=placed,
        out_specs=(P("seq", "head"), P("seq", "head")),
        check_vma=False,
    )
```

```python
import functools

import jax
import jax.numpy as jnp
from jax import lax
from jax.experimental import pallas as pl
from jax.experimental.pallas import tpu as pltpu
from jax.sharding import PartitionSpec as P

BLK = 128
GROUP = 5
BOTH = ("seq", "head")
MIB = 1 << 20


def attention_kernel(slot_ref, probs_ref, old_ref, near_ref, far_ref, new_ref, held, total, old, near, far, arrived, loaded):
    blocks, heads, topk = probs_ref.shape[:3]
    values = heads // GROUP

    def copy(q, k):
        at = q * topk + k
        return pltpu.make_async_copy(probs_ref.at[q, :, k], held.at[at], arrived.at[at])

    loads = [
        pltpu.make_async_copy(source, target, loaded.at[i])
        for i, (source, target) in enumerate(((near_ref, near), (far_ref, far), (old_ref, old)))
    ]
    for load in loads:
        load.start()
    for q in range(blocks):
        for k in range(topk):

            @pl.when(slot_ref[q * topk + k] >= 0)
            def _():
                copy(q, k).start()

    for load in loads:
        load.wait()
    total[...] = old[...].astype(jnp.float32)

    @pl.loop(0, blocks)
    def _(q):
        rows = pl.ds(pl.multiple_of(q * BLK, BLK), BLK)

        @pl.loop(0, topk)
        def _(k):
            slot = slot_ref[q * topk + k]

            @pl.when(slot >= 0)
            def _():
                copy(q, k).wait()
                place = lax.shift_right_logical(slot, 1)
                change = jnp.where(lax.bitwise_and(slot, 1) == 1, far[place], near[place])
                for v in range(values):
                    weights = held[q * topk + k, v * GROUP:(v + 1) * GROUP].reshape(GROUP * BLK, BLK)
                    part = jnp.dot(weights, change[:, v * BLK:(v + 1) * BLK], preferred_element_type=jnp.float32)
                    for g in range(GROUP):
                        at = (v * GROUP + g) * BLK
                        total[rows, at:at + BLK] += part[g * BLK:(g + 1) * BLK]

    new_ref[...] = total[...].astype(jnp.bfloat16)


def refresh(slots, cached_probs, out_old, near, far):
    blocks, heads, topk = cached_probs.shape[:3]
    near = near.reshape(-1, BLK, near.shape[-1])
    far = far.reshape(-1, BLK, far.shape[-1])
    return pl.pallas_call(
        attention_kernel,
        out_shape=jax.ShapeDtypeStruct(out_old.shape, jnp.bfloat16),
        in_specs=[pl.BlockSpec(memory_space=pltpu.SMEM)] + [pl.BlockSpec(memory_space=pl.ANY)] * 4,
        out_specs=pl.BlockSpec(memory_space=pltpu.VMEM),
        scratch_shapes=[
            pltpu.VMEM((blocks * topk, heads, BLK, BLK), jnp.bfloat16),
            pltpu.VMEM(out_old.shape, jnp.float32),
            pltpu.VMEM(out_old.shape, jnp.bfloat16),
            pltpu.VMEM(near.shape, jnp.bfloat16),
            pltpu.VMEM(far.shape, jnp.bfloat16),
            pltpu.SemaphoreType.DMA((blocks * topk,)),
            pltpu.SemaphoreType.DMA((3,)),
        ],
        compiler_params=pltpu.CompilerParams(vmem_limit_bytes=56 * MIB),
        cost_estimate=pl.CostEstimate(flops=MIB, bytes_accessed=MIB, transcendentals=0),
        name="attention",
    )(slots, cached_probs, out_old, near, far)


def product_kernel(count, pick_ref, new_ref, over_ref, other_ref, *refs):
    sources, out_ref, left, right, loaded = refs[:2 * count], *refs[2 * count:]
    depth = new_ref.shape[1]
    halves = (slice(0, depth), slice(depth, 2 * depth))

    def load_left(i, source):
        return pltpu.make_async_copy(source, left.at[:, halves[i]], loaded.at[i])

    load_left(1, other_ref).start()

    @pl.when(pick_ref[0] == 1)
    def _():
        load_left(0, new_ref).start()

    @pl.when(pick_ref[0] == 0)
    def _():
        load_left(0, over_ref).start()

    loads, column = [], 0
    for j in range(count):
        width = sources[2 * j].shape[1]
        for i in (0, 1):
            target = right.at[halves[i], column:column + width]
            loads.append(pltpu.make_async_copy(sources[2 * j + i], target, loaded.at[2 + 2 * j + i]))
            loads[-1].start()
        column += width
    load_left(0, over_ref).wait()
    load_left(1, other_ref).wait()
    for load in loads:
        load.wait()
    out_ref[...] = jnp.dot(left[...], right[...], preferred_element_type=jnp.float32).astype(jnp.bfloat16)


def product(pick, lefts, rights):
    rows, depth = lefts[0].shape
    width = sum(same.shape[1] for same, _ in rights)
    flat = [block for pair in rights for block in pair]
    return pl.pallas_call(
        functools.partial(product_kernel, len(rights)),
        out_shape=jax.ShapeDtypeStruct((rows, width), jnp.bfloat16),
        in_specs=[pl.BlockSpec(memory_space=pltpu.SMEM)]
        + [pl.BlockSpec(memory_space=pl.ANY)] * (len(lefts) + len(flat)),
        out_specs=pl.BlockSpec(memory_space=pltpu.VMEM),
        scratch_shapes=[
            pltpu.VMEM((rows, 2 * depth), jnp.bfloat16),
            pltpu.VMEM((2 * depth, width), jnp.bfloat16),
            pltpu.SemaphoreType.DMA((2 + len(flat),)),
        ],
        compiler_params=pltpu.CompilerParams(vmem_limit_bytes=56 * MIB),
        cost_estimate=pl.CostEstimate(flops=MIB, bytes_accessed=MIB, transcendentals=0),
        name="product",
    )(pick, *lefts, *flat)


def split_product_kernel(column, flag_ref, new_ref, over_ref, inner_ref, end_ref, keep_ref, *refs):
    *pass_refs, left, right, loaded = refs
    rows, width = new_ref.shape[0], end_ref.shape[1]

    def load_left(i, source):
        return pltpu.make_async_copy(source, left.at[i * rows:(i + 1) * rows], loaded.at[i])

    def load_right(source):
        return pltpu.make_async_copy(source, right, loaded.at[2])

    @pl.when(flag_ref[0] == 1)
    def _():
        load_left(0, new_ref).start()
        load_left(1, over_ref).start()

    @pl.when(flag_ref[0] == 0)
    def _():
        load_left(0, over_ref).start()
        load_left(1, new_ref).start()

    inner_part = inner_ref.at[:, column:column + width]

    @pl.when(flag_ref[1] == 1)
    def _():
        load_right(inner_part).start()

    @pl.when(flag_ref[1] == 0)
    def _():
        load_right(end_ref).start()

    load_right(end_ref).wait()
    load_left(0, new_ref).wait()
    load_left(1, new_ref).wait()
    both = jnp.dot(left[...], right[...], preferred_element_type=jnp.float32).astype(jnp.bfloat16)
    keep_ref[...] = both[:rows]
    for i, pass_ref in enumerate(pass_refs):
        piece = pass_ref.shape[1]
        pass_ref[...] = both[rows:, i * piece:(i + 1) * piece]


def split_product(flags, lefts, inner_block, end_block, column, piece):
    rows, depth = lefts[0].shape
    width = end_block.shape[1]
    return pl.pallas_call(
        functools.partial(split_product_kernel, column),
        out_shape=[jax.ShapeDtypeStruct((rows, width), jnp.bfloat16)]
        + [jax.ShapeDtypeStruct((rows, piece), jnp.bfloat16)] * (width // piece),
        in_specs=[pl.BlockSpec(memory_space=pltpu.SMEM)] + [pl.BlockSpec(memory_space=pl.ANY)] * 4,
        out_specs=[pl.BlockSpec(memory_space=pltpu.VMEM)] * (1 + width // piece),
        scratch_shapes=[
            pltpu.VMEM((2 * rows, depth), jnp.bfloat16),
            pltpu.VMEM((depth, width), jnp.bfloat16),
            pltpu.SemaphoreType.DMA((3,)),
        ],
        compiler_params=pltpu.CompilerParams(vmem_limit_bytes=56 * MIB),
        cost_estimate=pl.CostEstimate(flops=MIB, bytes_accessed=MIB, transcendentals=0),
        name="split_product",
    )(flags, *lefts, inner_block, end_block)


def add(a, b):
    return (a.astype(jnp.float32) + b.astype(jnp.float32)).astype(jnp.bfloat16)


def slots_of(key_lists, changed_block_numbers, me):
    count = changed_block_numbers.shape[0]
    places = jnp.bitwise_xor(jnp.arange(count, dtype=jnp.int32), me)
    hit = key_lists.reshape(-1)[:, None] == changed_block_numbers[None, :]
    return jnp.max(jnp.where(hit, places[None, :], -1), axis=1)


def local_any(cached_probs, out_old, key_lists, changed_block_numbers, delta_v, w_out):
    every = lax.all_gather(delta_v, "seq", axis=0, tiled=True)
    every = every.reshape(-1, 2, BLK, every.shape[-1])
    slots = slots_of(key_lists, changed_block_numbers, jnp.int32(0))
    attn_new = refresh(slots, cached_probs, out_old, every[:, 0], every[:, 1])
    terms = jnp.dot(
        attn_new, lax.all_gather(w_out, "seq", axis=1, tiled=True), preferred_element_type=jnp.float32
    )
    out_proj = lax.psum_scatter(terms.astype(jnp.bfloat16), "head", scatter_dimension=1, tiled=True)
    return attn_new, out_proj


def move(value, where):
    pairs = []
    for z in range(4):
        for x in range(2):
            for y in range(2):
                for c in range(2):
                    to = where(z, x, y, c)
                    if to is not None:
                        tz, tx, ty, tc = to
                        pairs.append((((z * 2 + x) * 2 + y) * 2 + c, ((tz * 2 + tx) * 2 + ty) * 2 + tc))
    return lax.ppermute(value, BOTH, pairs)


def inner(z):
    return z in (1, 2)


CUTS = (384, 256)


def columns(value, cuts=CUTS):
    at, parts = 0, []
    for width in cuts:
        parts.append(value[:, at:at + width])
        at += width
    return parts


def tie(*values):
    return lax.optimization_barrier(values)


def local_line(cached_probs, out_old, key_lists, changed_block_numbers, delta_v, w_out):
    s, h = lax.axis_index("seq"), lax.axis_index("head")
    z, x, y, c = s // 2, s % 2, h // 2, h % 2
    half = z // 2
    is_inner = (z == 1) | (z == 2)

    def to_core(value):
        return move(value, lambda z, x, y, c: (z, x, y, 1 - c))

    def to_pair(value):
        return move(value, lambda z, x, y, c: (z ^ 1, x, y, c))

    def to_cross(value):
        return move(value, lambda z, x, y, c: (3 - z, x, y, c) if inner(z) else (z, x, y, 1 - c))

    def to_far_end(value):
        return move(value, lambda z, x, y, c: (z ^ 2 if inner(z) else z ^ 1, x, y, c))

    line = [move(delta_v, lambda z, x, y, c, k=k: (z ^ k, x, y, c)) for k in (1, 2, 3)]
    near = jnp.concatenate([delta_v] + line, axis=0)
    far = move(near, lambda z, x, y, c: (z, 1 - x, y, c))
    pair, cross = to_pair(w_out), to_cross(w_out)
    cross_end = to_pair(cross)
    last = to_cross(pair)

    slots = slots_of(key_lists, changed_block_numbers, s.astype(jnp.int32))
    attn_new = refresh(slots, cached_probs, out_old, near, far)
    over_x = move(attn_new, lambda z, x, y, c: (z, 1 - x, y, c))
    other = to_core(jnp.where(x == c, over_x, attn_new))
    pick = (x == c).astype(jnp.int32).reshape(1)
    flags = jnp.stack([x == c, is_inner]).astype(jnp.int32)
    rows = [attn_new, over_x, other]

    def with_other(block):
        return block, to_core(block)

    def both_cores(inner_block, end_block, column):
        kept, *passed = split_product(flags, rows[:2], inner_block, end_block, column, BLK if column == 0 else end_block.shape[1])
        return add(kept, jnp.concatenate([to_core(v) for v in passed], axis=1))

    def to_sum(p_half, p_cross):
        return jnp.where(y == half, p_cross, p_half), jnp.where(y == half, p_half, p_cross)

    def summed(sent, kept):
        return add(kept, move(sent, lambda z, x, y, c: (z, x, 1 - y, c)))

    p_half = product(pick, rows, [with_other(v) for v in (w_out, pair)])
    p_own, p_pair = columns(p_half, (w_out.shape[1], w_out.shape[1]))
    parts = columns(pair)
    parts[0], p_half, last, cross_end = tie(parts[0], p_half, last, cross_end)
    block = jnp.where(is_inner, cross, cross_end)
    p_cross = product(pick, rows, [with_other(v) for v in columns(block)])
    last_end = [to_far_end(parts[0])]
    parts[1], block = tie(parts[1], block)
    last_end.append(to_far_end(parts[1]))
    first = summed(*to_sum(p_own, p_cross))
    last_end[0], first = tie(last_end[0], first)
    first = columns(first)
    second, terms, column = [], None, 0
    for p_pair, end_part in zip(columns(p_pair), last_end, strict=True):
        if terms:
            *terms, end_part = tie(*terms, end_part)
            second.append(summed(*terms))
        p_last = both_cores(last, end_part, column)
        column += end_part.shape[1]
        if second:
            second[0], p_last = tie(second[0], p_last)
        terms = to_sum(p_pair, p_last)
    second.append(summed(*terms))

    first_core = jnp.where(y == half, z % 2, half)
    out = []
    for mine, other in zip(first, second, strict=True):
        for_core = [jnp.where(first_core == j, mine, other) for j in (0, 1)]
        by_same = move(
            jnp.where(x == 0, for_core[0], for_core[1]),
            lambda z, x, y, c: (z, x, 1 - y, c) if x == c else (z, c, y, x),
        )
        by_other = move(
            jnp.where(x == 0, for_core[1], for_core[0]), lambda z, x, y, c: (z, c, y, 1 - x)
        )
        stays = jnp.where(c == 0, for_core[0], for_core[1])
        out.append((jnp.where(x == c, stays, by_same), by_other))
    left = jnp.concatenate([jnp.where(c == 0, a, b) for a, b in out], axis=1)
    right = jnp.concatenate([jnp.where(c == 0, b, a) for a, b in out], axis=1)
    return attn_new, jnp.concatenate([left, right], axis=1)


def solution(mesh):
    placed = (
        P("seq", "head", None, None, None),
        P("seq", "head"),
        P("seq", None),
        P(),
        P("seq", "head"),
        P("head", "seq"),
    )
    on_line = mesh.shape["seq"] == 8 and mesh.shape["head"] == 4
    return jax.shard_map(
        local_line if on_line else local_any,
        mesh=mesh,
        in_specs=placed,
        out_specs=(P("seq", "head"), P("seq", "head")),
        check_vma=False,
    )
```
